32 devices in a mesh: vocab: 8 (over z, x), hid: 4 (over y, core).
Axes of the slice: x: 2, y: 2, z: 4, core: 2. Of those that a mesh axis runs over, the one named last changes fastest.
Arguments:
- student_hidden: bfloat16 [1024, 8192], P(None, 'hid'), as said below
- head_weight: bfloat16 [8192, 16384], P('hid', 'vocab'), as said below
- teacher_logits: bfloat16 [1024, 16384], P(('vocab', 'hid')), as said below
Outputs:
- loss_value: float32 [], replicated
- grad_hidden: bfloat16 [1024, 8192], P('vocab', 'hid')
- grad_weight: bfloat16 [8192, 16384], P('hid', 'vocab')
Inputs may be any that keep to these rules, and one draw needn't show every extreme that they name: `student_hidden`: hidden states of order one to some tens. `head_weight`: weights of order one over the square root of 8192. `teacher_logits`: logits of order one to some hundreds.
All inputs are finite; a program needn't handle non-finite values.
Results may differ from the reference program's by a relative error of at most 0.02055.
Values may be sent and summed in bfloat16 or wider, within the bound.
A program may use at most 128 MiB of HBM per device.

```python
import jax
import jax.numpy as jnp
from jax import lax

D = 8192
TOKENS = 1024
V = 16384


def draw_head_weight(key, part):
    key = jax.random.fold_in(key, 11)
    weight = jax.random.normal(key, (D, V), jnp.float32) * D ** (-0.5)
    return weight.astype(jnp.bfloat16)


def draw_student_hidden(key, part):
    key = jax.random.fold_in(key, 12)
    hidden = 3.0 * jax.random.truncated_normal(key, -4.0, 4.0, (TOKENS, D), jnp.float32)
    return hidden.astype(jnp.bfloat16)


def draw_teacher_logits(key, part):
    key = jax.random.fold_in(key, 13)
    key_val = jax.random.fold_in(key, 0)
    logits = 3.0 * jax.random.truncated_normal(key_val, -4.0, 4.0, (TOKENS, V), jnp.float32)
    return logits.astype(jnp.bfloat16)


def setup_inputs(seed: int = 0) -> dict:
    key_of = jax.random.split(jax.random.key(seed), 4)
    student_hidden = draw_student_hidden(jax.random.fold_in(key_of[3], 71), 0)
    head_weight = draw_head_weight(jax.random.fold_in(key_of[3], 71), 0)
    teacher_logits = draw_teacher_logits(jax.random.fold_in(key_of[3], 71), 0)
    return dict(student_hidden=student_hidden, head_weight=head_weight, teacher_logits=teacher_logits)


def log_softmax_rows(values):
    top_value = jnp.max(values, axis=1, keepdims=True)
    total = jnp.sum(jnp.exp(values - top_value), axis=1, keepdims=True)
    return values - top_value - jnp.log(total)


def reference(student_hidden, head_weight, teacher_logits):
    logits = jnp.dot(student_hidden, head_weight, preferred_element_type=jnp.float32)
    student_log = log_softmax_rows(logits)
    teacher_log = log_softmax_rows(teacher_logits.astype(jnp.float32))
    probs = jnp.exp(student_log)
    log_ratio = student_log - teacher_log
    kl_row = jnp.sum(probs * log_ratio, axis=1, keepdims=True)
    loss_value = jnp.sum(kl_row) / TOKENS
    grad_logits = (probs * (log_ratio - kl_row) / TOKENS).astype(jnp.bfloat16)
    grad_hidden = lax.dot_general(grad_logits, head_weight, (((1,), (1,)), ((), ())), preferred_element_type=jnp.float32).astype(jnp.bfloat16)
    grad_weight = lax.dot_general(student_hidden, grad_logits, (((0,), (0,)), ((), ())), preferred_element_type=jnp.float32).astype(jnp.bfloat16)
    return (loss_value, grad_hidden, grad_weight)
```

```python
import jax
import jax.numpy as jnp
from jax import lax
from jax.sharding import PartitionSpec as P


def shards(student_hidden, head_weight, teacher_logits):
    n_vocab = lax.axis_size("vocab")
    n_hid = lax.axis_size("hid")
    tokens, width = student_hidden.shape
    vocab_width = head_weight.shape[1]
    per_dev = teacher_logits.shape[0]
    mine = n_vocab * per_dev
    teacher = lax.all_to_all(
        teacher_logits, "vocab", split_axis=1, concat_axis=0, tiled=True
    ).astype(jnp.float32)
    hidden = student_hidden.reshape(n_vocab, n_hid, per_dev, width)
    hidden = hidden.transpose(1, 0, 2, 3).reshape(tokens, width)
    partial_value = jnp.dot(hidden, head_weight, preferred_element_type=jnp.float32)
    logits = lax.psum_scatter(partial_value, "hid", scatter_dimension=0, tiled=True)
    top_s = jnp.max(logits, axis=1, keepdims=True)
    top_t = jnp.max(teacher, axis=1, keepdims=True)
    e = jnp.exp(logits - top_s)
    stats = jnp.stack(
        [
            top_s[:, 0],
            jnp.sum(e, axis=1),
            jnp.sum(e * ((logits - top_s) - (teacher - top_t)), axis=1),
            top_t[:, 0],
            jnp.sum(jnp.exp(teacher - top_t), axis=1),
        ]
    )
    every = lax.all_gather(stats, "vocab", axis=0)
    m_s, s_s, a, m_t, s_t = [every[:, i] for i in range(5)]
    all_s, all_t = jnp.max(m_s, axis=0), jnp.max(m_t, axis=0)
    w = jnp.exp(m_s - all_s)
    total_s = jnp.sum(w * s_s, axis=0)
    total_t = jnp.sum(jnp.exp(m_t - all_t) * s_t, axis=0)
    log_s, log_t = jnp.log(total_s), jnp.log(total_t)
    gap = (m_s - all_s) - (m_t - all_t)
    kl_row = jnp.sum(w * (a + s_s * gap), axis=0) / total_s - log_s + log_t
    loss_value = lax.psum(jnp.sum(kl_row), "hid") / tokens
    student_log = logits - (all_s + log_s)[:, None]
    teacher_log = teacher - (all_t + log_t)[:, None]
    grad = (jnp.exp(student_log) * (student_log - teacher_log - kl_row[:, None]) / tokens).astype(
        jnp.bfloat16
    )
    grad = lax.all_gather(grad, "hid", axis=0, tiled=True)
    grad_hidden = lax.dot_general(
        grad, head_weight, (((1,), (1,)), ((), ())), preferred_element_type=jnp.float32
    ).astype(jnp.bfloat16)
    grad_hidden = grad_hidden.reshape(n_hid, n_vocab, per_dev, width).transpose(1, 0, 2, 3)
    grad_hidden = lax.psum_scatter(
        grad_hidden.reshape(tokens, width), "vocab", scatter_dimension=0, tiled=True
    )
    grad_weight = lax.dot_general(
        hidden, grad, (((0,), (0,)), ((), ())), preferred_element_type=jnp.float32
    ).astype(jnp.bfloat16)
    return (loss_value, grad_hidden, grad_weight)


def solution(mesh):
    in_specs = (P(None, "hid"), P("hid", "vocab"), P(("vocab", "hid"), None))
    out_specs = (P(), P("vocab", "hid"), P("hid", "vocab"))
    return jax.shard_map(shards, mesh=mesh, in_specs=in_specs, out_specs=out_specs, check_vma=False)
```

```python
import functools

import jax
import jax.numpy as jnp
from jax import lax
from jax.experimental import pallas as pl
from jax.experimental.pallas import tpu as pltpu
from jax.sharding import PartitionSpec as P


F32, BF16 = jnp.float32, jnp.bfloat16
HI, LO = 4095.0, 2047.0


def fused(
    tokens, hid, wgt, teach, loss_o, gh_o, gw_o,
    W, H, T, SC, RC, SY, RY, XF, LG, STS, STR, TB, KLS, KLR, G, RT, GHS, GHR, GHK, ZS, ZR, GWS,
    ld, t_s, t_r, c_s, c_r, y_s, y_r, st_s, st_r, g_s, g_r, kl_s, kl_r, x_s, x_r, z_s, z_r, gw_s,
):
    nv, nh, per, width = hid.shape
    vw = wgt.shape[1]
    half = per // 2
    rows = nv * half
    nz, ncb = nv // 2, GHS.shape[0] // 2
    cw = width // ncb
    nt = vw // 4
    hv = vw // 2
    me_v, me_h = lax.axis_index("vocab"), lax.axis_index("hid")
    y, c = me_h // 2, me_h % 2
    z, x = me_v // 2, me_v % 2
    h_core, h_y, h_far = 2 * y + 1 - c, 2 * (1 - y) + c, 2 * (1 - y) + 1 - c

    def remote(src, dst, send, recv, v, h):
        return pltpu.make_async_remote_copy(
            src_ref=src, dst_ref=dst, send_sem=send, recv_sem=recv,
            device_id={"vocab": v, "hid": h}, device_id_type=pl.DeviceIdType.MESH,
        )

    loads = [
        pltpu.make_async_copy(hid.at[:, h, pl.ds(th * half, half), :], H.at[h, th], ld.at[2 * h + th])
        for h in range(nh) for th in range(2)
    ]
    loads.append(pltpu.make_async_copy(wgt, W, ld.at[2 * nh]))
    for copy in loads:
        copy.start()

    def teach_part(th, v):
        return teach.at[pl.ds(th * half, half), pl.ds(pl.multiple_of(v * vw, vw), vw)]

    own_t = [
        pltpu.make_async_copy(teach_part(th, me_v), T.at[th, me_v], ld.at[2 * nh + 1 + th]) for th in range(2)
    ]
    for copy in own_t:
        copy.start()

    barrier = pltpu.get_barrier_semaphore()
    for h in (h_core, h_y, h_far):
        pl.semaphore_signal(
            barrier, inc=1, device_id={"vocab": me_v, "hid": h}, device_id_type=pl.DeviceIdType.MESH
        )
    for k in range(1, nv):
        pl.semaphore_signal(
            barrier, inc=1, device_id={"vocab": (me_v + k) % nv, "hid": me_h},
            device_id_type=pl.DeviceIdType.MESH,
        )
    pl.semaphore_wait(barrier, nh - 1 + nv - 1)

    def send_t(th, k):
        v = (me_v + k) % nv
        return remote(teach_part(th, v), T.at[th, me_v], t_s.at[th, k], t_r.at[th, k], v, me_h)

    for th in range(2):
        for k in range(1, nv):
            send_t(th, k).start()
    for copy in loads:
        copy.wait()

    def project(h, out):
        @pl.loop(0, vw // nt)
        def _(i):
            cols = pl.ds(pl.multiple_of(i * nt, nt), nt)
            r = jnp.dot(H[h].reshape(2 * rows, width), W[:, cols], preferred_element_type=F32)
            out[:, :, cols] = r.reshape(2, rows, nt)

    def core_copy(kind, th):
        return remote(
            SC.at[kind, th], RC.at[kind, th], c_s.at[kind, th], c_r.at[kind, th], me_v, h_core
        )

    def y_copy(th):
        return remote(SY.at[th], RY.at[th], y_s.at[th], y_r.at[th], me_v, h_y)

    project(h_far, SC.at[0])
    for th in range(2):
        core_copy(0, th).start()
    project(h_y, XF)
    for th in range(2):
        core_copy(0, th).wait_recv()

        @pl.loop(0, nv)
        def _(i):
            r16 = pl.ds(pl.multiple_of(i * half, half), half)
            s = XF[th, r16] + RC[0, th, r16]
            top = jnp.maximum(jnp.max(jnp.abs(s), axis=1, keepdims=True), 1e-20)
            hi = jnp.floor(s[:, :hv] * (HI / top) + 0.5)
            lo = jnp.floor(s[:, hv:] * (LO / top) + 0.5)
            SY[th, r16, pl.ds(0, hv)] = hi * 4096.0 + lo
            SY[th, r16, pl.ds(hv, 128)] = jnp.broadcast_to(top, (half, 128))

        y_copy(th).start()
    project(h_core, SC.at[1])
    for th in range(2):
        core_copy(1, th).start()
    project(me_h, LG)

    lane = lax.broadcasted_iota(jnp.int32, (half, rows), 1)
    KLS[...] = jnp.zeros_like(KLS)

    def st_copy(th, k):
        return remote(
            STS.at[th], STR.at[th, me_v], st_s.at[th, k], st_r.at[th, k], (me_v + k) % nv, me_h
        )

    def stats(th):
        core_copy(1, th).wait_recv()
        y_copy(th).wait_recv()
        own_t[th].wait()
        for k in range(1, nv):
            send_t(th, k).wait_recv()

        @pl.loop(0, nv)
        def _(i):
            r16 = pl.ds(pl.multiple_of(i * half, half), half)
            f = RY[th, r16, pl.ds(0, hv)]
            top = RY[th, r16, pl.ds(hv, 128)][:, 0:1]
            hi = jnp.floor(f * (1.0 / 4096.0) + 0.5)
            lo = f - hi * 4096.0
            both = jnp.concatenate([hi * (top / HI), lo * (top / LO)], axis=1)
            l = LG[th, r16] + RC[1, th, r16] + both
            LG[th, r16] = l
            t = T[th, i].astype(F32)
            m = jnp.max(l, axis=1, keepdims=True)
            mt = jnp.max(t, axis=1, keepdims=True)
            l, t = l - m, t - mt
            e = jnp.exp(l)
            cols = [
                m, jnp.sum(e, axis=1, keepdims=True), jnp.sum(e * (l - t), axis=1, keepdims=True),
                mt, jnp.sum(jnp.exp(t), axis=1, keepdims=True),
            ]
            block = jnp.zeros((half, rows), F32)
            for j, col in enumerate(cols):
                block = jnp.where(lane == j, col, block)
            TB[r16, :] = block

        flat = TB[...].T[0:8]
        STS[th] = flat
        STR[th, me_v] = flat
        for k in range(1, nv):
            st_copy(th, k).start()

    def g_copy(th, which):
        if which == 0:
            return remote(G.at[me_h, th], G.at[me_h, th], g_s.at[th, 0], g_r.at[th, 0], me_v, h_core)
        if which == 1:
            return remote(G.at[me_h, th], G.at[me_h, th], g_s.at[th, 1], g_r.at[th, 1], me_v, h_y)
        return remote(G.at[h_y, th], G.at[h_y, th], g_s.at[th, 2], g_r.at[th, 2], me_v, h_core)

    def grad(th):
        for k in range(1, nv):
            st_copy(th, k).wait_recv()
        p = [STR[th, d] for d in range(nv)]
        m_s, s_s, a, m_t, s_t = [[q[j : j + 1] for q in p] for j in range(5)]
        top_s, top_t = functools.reduce(jnp.maximum, m_s), functools.reduce(jnp.maximum, m_t)
        total_s = total_t = total_a = jnp.zeros_like(top_s)
        for d in range(nv):
            w = jnp.exp(m_s[d] - top_s)
            total_s = total_s + w * s_s[d]
            total_t = total_t + jnp.exp(m_t[d] - top_t) * s_t[d]
            total_a = total_a + w * (a[d] + s_s[d] * ((m_s[d] - top_s) - (m_t[d] - top_t)))
        log_s, log_t = jnp.log(total_s), jnp.log(total_t)
        kl = total_a / total_s - log_s + log_t
        KLS[th : th + 1, :] = kl
        TB[0:1, :] = top_s + log_s
        TB[1:2, :] = top_t + log_t
        TB[2:3, :] = kl
        TB[...] = TB[...].T

        @pl.loop(0, nv)
        def _(i):
            r16 = pl.ds(pl.multiple_of(i * half, half), half)
            b = TB[r16, :]
            u = LG[th, r16] - b[:, 0:1]
            gap = u - (T[th, i].astype(F32) - b[:, 1:2])
            G[me_h, th, r16] = (jnp.exp(u) * (gap - b[:, 2:3]) / tokens).astype(BF16)

        g_copy(th, 1).start()
        g_copy(th, 0).start()

    def kl_copy(k):
        return remote(KLS, KLR.at[me_h], kl_s.at[k], kl_r.at[k], me_v, (me_h + k) % nh)

    stats(0)
    grad(0)
    stats(1)
    grad(1)
    KLR[me_h] = KLS[...]
    for k in range(1, nh):
        kl_copy(k).start()

    def x_copy(s):
        return remote(GHS.at[s], GHR.at[s], x_s.at[s], x_r.at[s], 2 * z + 1 - x, me_h)

    def z_copy(s, k):
        to = (z + k) % nz
        return remote(ZS.at[s, to], ZR.at[s, z], z_s.at[s, k], z_r.at[s, k], 2 * to + x, me_h)

    def hidden_part(th):
        g_copy(th, 1).wait_recv()
        g_copy(th, 2).start()
        g_copy(th, 0).wait_recv()
        g_copy(th, 2).wait_recv()

        @pl.loop(0, ncb)
        def _(cb):
            s = th * ncb + cb
            r = lax.dot_general(
                G[:, th].reshape(nh * rows, vw), W[pl.ds(pl.multiple_of(cb * cw, cw), cw), :],
                (((1,), (1,)), ((), ())), preferred_element_type=F32,
            )
            RT[...] = r.reshape(nh, nz, 2, half, cw)
            GHS[s] = RT[:, :, 1 - x].astype(BF16)
            x_copy(s).start()
            GHK[s] = RT[:, :, x]

    def pass_on(s):
        x_copy(s).wait_recv()
        for to in range(nz):
            ZS[s, to] = (GHK[s, :, to] + GHR[s, :, to].astype(F32)).astype(BF16)
        for k in range(1, nz):
            z_copy(s, k).start()

    tile = width // 8

    def gw_copy(i, slot):
        return pltpu.make_async_copy(
            GWS.at[slot], gw_o.at[pl.ds(pl.multiple_of(i * tile, tile), tile), :], gw_s.at[slot]
        )

    def weight_tile(i):
        slot = i % 2

        @pl.when(i >= 2)
        def _():
            gw_copy(i - 2, slot).wait()

        h = H[:, :, :, :, pl.ds(pl.multiple_of(i * tile, tile), tile)].reshape(2 * nh * rows, tile)

        @pl.loop(0, vw // nt)
        def _(j):
            cols = pl.ds(pl.multiple_of(j * nt, nt), nt)
            GWS[slot, :, cols] = lax.dot_general(
                h, G[:, :, :, cols].reshape(2 * nh * rows, nt),
                (((0,), (0,)), ((), ())), preferred_element_type=F32,
            ).astype(BF16)

        gw_copy(i, slot).start()

    hidden_part(0)
    pass_on(0)
    pass_on(1)
    hidden_part(1)

    @pl.loop(0, 8)
    def _(i):
        weight_tile(i)

        @pl.when(i < 2 * ncb - 2)
        def _():
            pass_on(i + 2)

    for i in (6, 7):
        gw_copy(i, i % 2).wait()
    for th in range(2):
        @pl.loop(0, ncb)
        def _(cb):
            s = th * ncb + cb
            total = ZS[s, z].astype(F32)
            for k in range(1, nz):
                z_copy(s, k).wait_recv()
                total = total + ZR[s, (z + nz - k) % nz].astype(F32)
            cols = pl.ds(pl.multiple_of(cb * cw, cw), cw)
            gh_o[:, pl.ds(th * half, half), cols] = total.astype(BF16)
            x_copy(s).wait_send()
            for k in range(1, nz):
                z_copy(s, k).wait_send()

    for k in range(1, nh):
        kl_copy(k).wait()
    kl_all = functools.reduce(jnp.add, [KLR[h] for h in range(nh)])
    kl_all = jnp.sum(jnp.sum(kl_all, axis=1, keepdims=True), axis=0, keepdims=True) / tokens
    loss_o[...] = jnp.broadcast_to(kl_all, loss_o.shape)
    for th in range(2):
        y_copy(th).wait_send()
        for kind in range(2):
            core_copy(kind, th).wait_send()
        for which in range(3):
            g_copy(th, which).wait_send()
        for k in range(1, nv):
            send_t(th, k).wait_send()
            st_copy(th, k).wait_send()


def fused_shards(student_hidden, head_weight, teacher_logits):
    nv, nh = lax.axis_size("vocab"), lax.axis_size("hid")
    tokens, width = student_hidden.shape
    vw = head_weight.shape[1]
    per = teacher_logits.shape[0]
    half, nz, ncb = per // 2, nv // 2, 4
    rows, cw, tile = nv * half, width // ncb, width // 8
    hidden = student_hidden.reshape(nv, nh, per, width)
    any_, vmem = pl.BlockSpec(memory_space=pl.ANY), pl.BlockSpec(memory_space=pltpu.VMEM)
    dma = lambda *shape: pltpu.SemaphoreType.DMA(shape)
    steps = 2 * ncb
    loss, gh, gw = pl.pallas_call(
        functools.partial(fused, tokens),
        out_shape=(
            jax.ShapeDtypeStruct((8, 128), F32),
            jax.ShapeDtypeStruct((nh, per, width), BF16),
            jax.ShapeDtypeStruct((width, vw), BF16),
        ),
        in_specs=[any_, any_, any_],
        out_specs=(vmem, vmem, any_),
        scratch_shapes=[
            pltpu.VMEM((width, vw), BF16),
            pltpu.VMEM((nh, 2, nv, half, width), BF16),
            pltpu.VMEM((2, nv, half, vw), BF16),
            pltpu.VMEM((2, 2, rows, vw), F32),
            pltpu.VMEM((2, 2, rows, vw), F32),
            pltpu.VMEM((2, rows, vw // 2 + 128), F32),
            pltpu.VMEM((2, rows, vw // 2 + 128), F32),
            pltpu.VMEM((2, rows, vw), F32),
            pltpu.VMEM((2, rows, vw), F32),
            pltpu.VMEM((2, 8, rows), F32),
            pltpu.VMEM((2, nv, 8, rows), F32),
            pltpu.VMEM((rows, rows), F32),
            pltpu.VMEM((8, rows), F32),
            pltpu.VMEM((nh, 8, rows), F32),
            pltpu.VMEM((nh, 2, rows, vw), BF16),
            pltpu.VMEM((nh, nz, 2, half, cw), F32),
            pltpu.VMEM((steps, nh, nz, half, cw), BF16),
            pltpu.VMEM((steps, nh, nz, half, cw), BF16),
            pltpu.VMEM((steps, nh, nz, half, cw), F32),
            pltpu.VMEM((steps, nz, nh, half, cw), BF16),
            pltpu.VMEM((steps, nz, nh, half, cw), BF16),
            pltpu.VMEM((2, tile, vw), BF16),
            dma(2 * nh + 3),
            dma(2, nv), dma(2, nv), dma(2, 2), dma(2, 2), dma(2), dma(2), dma(2, nv), dma(2, nv),
            dma(2, 3), dma(2, 3), dma(nh), dma(nh), dma(steps), dma(steps), dma(steps, nz), dma(steps, nz),
            dma(2),
        ],
        compiler_params=pltpu.CompilerParams(
            collective_id=0, has_side_effects=True, vmem_limit_bytes=60 * 1024 * 1024
        ),
        cost_estimate=pl.CostEstimate(
            flops=6 * tokens * width * vw, bytes_accessed=4 * width * vw, transcendentals=0
        ),
    )(hidden, head_weight, teacher_logits)
    return loss[0, 0], gh.reshape(nh * per, width), gw


def shards(student_hidden, head_weight, teacher_logits):
    n_vocab = lax.axis_size("vocab")
    n_hid = lax.axis_size("hid")
    tokens, width = student_hidden.shape
    vocab_width = head_weight.shape[1]
    per_dev = teacher_logits.shape[0]
    mine = n_vocab * per_dev
    teacher = lax.all_to_all(
        teacher_logits, "vocab", split_axis=1, concat_axis=0, tiled=True
    ).astype(jnp.float32)
    hidden = student_hidden.reshape(n_vocab, n_hid, per_dev, width)
    hidden = hidden.transpose(1, 0, 2, 3).reshape(tokens, width)
    partial_value = jnp.dot(hidden, head_weight, preferred_element_type=jnp.float32)
    logits = lax.psum_scatter(partial_value, "hid", scatter_dimension=0, tiled=True)
    top_s = jnp.max(logits, axis=1, keepdims=True)
    top_t = jnp.max(teacher, axis=1, keepdims=True)
    e = jnp.exp(logits - top_s)
    stats = jnp.stack(
        [
            top_s[:, 0],
            jnp.sum(e, axis=1),
            jnp.sum(e * ((logits - top_s) - (teacher - top_t)), axis=1),
            top_t[:, 0],
            jnp.sum(jnp.exp(teacher - top_t), axis=1),
        ]
    )
    every = lax.all_gather(stats, "vocab", axis=0)
    m_s, s_s, a, m_t, s_t = [every[:, i] for i in range(5)]
    all_s, all_t = jnp.max(m_s, axis=0), jnp.max(m_t, axis=0)
    w = jnp.exp(m_s - all_s)
    total_s = jnp.sum(w * s_s, axis=0)
    total_t = jnp.sum(jnp.exp(m_t - all_t) * s_t, axis=0)
    log_s, log_t = jnp.log(total_s), jnp.log(total_t)
    gap = (m_s - all_s) - (m_t - all_t)
    kl_row = jnp.sum(w * (a + s_s * gap), axis=0) / total_s - log_s + log_t
    loss_value = lax.psum(jnp.sum(kl_row), "hid") / tokens
    student_log = logits - (all_s + log_s)[:, None]
    teacher_log = teacher - (all_t + log_t)[:, None]
    grad = (jnp.exp(student_log) * (student_log - teacher_log - kl_row[:, None]) / tokens).astype(
        jnp.bfloat16
    )
    grad = lax.all_gather(grad, "hid", axis=0, tiled=True)
    grad_hidden = lax.dot_general(
        grad, head_weight, (((1,), (1,)), ((), ())), preferred_element_type=jnp.float32
    ).astype(jnp.bfloat16)
    grad_hidden = grad_hidden.reshape(n_hid, n_vocab, per_dev, width).transpose(1, 0, 2, 3)
    grad_hidden = lax.psum_scatter(
        grad_hidden.reshape(tokens, width), "vocab", scatter_dimension=0, tiled=True
    )
    grad_weight = lax.dot_general(
        hidden, grad, (((0,), (0,)), ((), ())), preferred_element_type=jnp.float32
    ).astype(jnp.bfloat16)
    return (loss_value, grad_hidden, grad_weight)


def solution(mesh):
    fits = mesh.shape["hid"] == 4 and mesh.shape["vocab"] == 8
    def body(student_hidden, head_weight, teacher_logits):
        ok = fits and teacher_logits.shape[0] == 32
        return (fused_shards if ok else shards)(student_hidden, head_weight, teacher_logits)

    in_specs = (P(None, "hid"), P("hid", "vocab"), P(("vocab", "hid"), None))
    out_specs = (P(), P("vocab", "hid"), P("hid", "vocab"))
    return jax.shard_map(body, mesh=mesh, in_specs=in_specs, out_specs=out_specs, check_vma=False)
```

```python
import functools

import jax
import jax.numpy as jnp
from jax import lax
from jax.experimental import pallas as pl
from jax.experimental.pallas import tpu as pltpu
from jax.sharding import PartitionSpec as P


F32, BF16 = jnp.float32, jnp.bfloat16
HI, LO = 4095.0, 2047.0


def fused(
    tokens, hid, wgt, teach, loss_o, gh_o, gw_o,
    W, H, T, SC, RC, SY, RY, XF, LG, STS, STR, TB, KLS, KLR, G, RT, GHS, GHR, GHK, ZS, ZR, GWS,
    ld, t_s, t_r, c_s, c_r, y_s, y_r, st_s, st_r, g_s, g_r, kl_s, kl_r, x_s, x_r, z_s, z_r, gw_s,
):
    nv, nh, per, width = hid.shape
    vw = wgt.shape[1]
    half = per // 2
    rows = nv * half
    nz, ncb = nv // 2, GHS.shape[0] // 2
    cw = width // ncb
    nt = vw // 4
    hv = vw // 2
    me_v, me_h = lax.axis_index("vocab"), lax.axis_index("hid")
    y, c = me_h // 2, me_h % 2
    z, x = me_v // 2, me_v % 2
    h_core, h_y, h_far = 2 * y + 1 - c, 2 * (1 - y) + c, 2 * (1 - y) + 1 - c

    def remote(src, dst, send, recv, v, h):
        return pltpu.make_async_remote_copy(
            src_ref=src, dst_ref=dst, send_sem=send, recv_sem=recv,
            device_id={"vocab": v, "hid": h}, device_id_type=pl.DeviceIdType.MESH,
        )

    def load_h(k, th):
        h = (h_far, h_y, h_core, me_h)[k]
        return pltpu.make_async_copy(
            hid.at[:, h, pl.ds(th * half, half), :], H.at[h, th], ld.at[2 * k + th]
        )

    def load_w(i):
        cols = pl.ds(pl.multiple_of(i * nt, nt), nt)
        return pltpu.make_async_copy(wgt.at[:, cols], W.at[:, cols], ld.at[2 * nh + 2 + i])

    for k in range(nh):
        for th in range(2):
            load_h(k, th).start()
        if k == 0:
            for i in range(vw // nt):
                load_w(i).start()

    def teach_part(th, v):
        return teach.at[pl.ds(th * half, half), pl.ds(pl.multiple_of(v * vw, vw), vw)]

    own_t = [
        pltpu.make_async_copy(teach_part(th, me_v), T.at[th, me_v], ld.at[2 * nh + th]) for th in range(2)
    ]
    for copy in own_t:
        copy.start()

    barrier = pltpu.get_barrier_semaphore()
    for h in (h_core, h_y, h_far):
        pl.semaphore_signal(
            barrier, inc=1, device_id={"vocab": me_v, "hid": h}, device_id_type=pl.DeviceIdType.MESH
        )
    for k in range(1, nv):
        pl.semaphore_signal(
            barrier, inc=1, device_id={"vocab": (me_v + k) % nv, "hid": me_h},
            device_id_type=pl.DeviceIdType.MESH,
        )
    pl.semaphore_wait(barrier, nh - 1 + nv - 1)

    def send_t(th, k):
        v = (me_v + k) % nv
        return remote(teach_part(th, v), T.at[th, me_v], t_s.at[th, k], t_r.at[th, k], v, me_h)

    for k in range(1, nv):
        send_t(0, k).start()

    def project(k, out):
        h = (h_far, h_y, h_core, me_h)[k]
        for th in range(2):
            load_h(k, th).wait()

        @pl.loop(0, vw // nt)
        def _(i):
            if k == 0:
                load_w(i).wait()
            cols = pl.ds(pl.multiple_of(i * nt, nt), nt)
            r = jnp.dot(H[h].reshape(2 * rows, width), W[:, cols], preferred_element_type=F32)
            out[:, :, cols] = r.reshape(2, rows, nt)

    def core_copy(kind, th):
        return remote(
            SC.at[kind, th], RC.at[kind, th], c_s.at[kind, th], c_r.at[kind, th], me_v, h_core
        )

    def y_copy(th):
        return remote(SY.at[th], RY.at[th], y_s.at[th], y_r.at[th], me_v, h_y)

    project(0, SC.at[0])
    for th in range(2):
        core_copy(0, th).start()
    project(1, XF)
    for th in range(2):
        core_copy(0, th).wait_recv()

        @pl.loop(0, nv)
        def _(i):
            r16 = pl.ds(pl.multiple_of(i * half, half), half)
            s = XF[th, r16] + RC[0, th, r16]
            top = jnp.maximum(jnp.max(jnp.abs(s), axis=1, keepdims=True), 1e-20)
            hi = jnp.floor(s[:, :hv] * (HI / top) + 0.5)
            lo = jnp.floor(s[:, hv:] * (LO / top) + 0.5)
            SY[th, r16, pl.ds(0, hv)] = hi * 4096.0 + lo
            SY[th, r16, pl.ds(hv, 128)] = jnp.broadcast_to(top, (half, 128))

        if th == 0:
            y_copy(0).start()
    project(2, SC.at[1])
    for th in range(2):
        core_copy(1, th).start()
    project(3, LG)
    for k in range(1, nv):
        send_t(1, k).start()

    lane = lax.broadcasted_iota(jnp.int32, (half, rows), 1)
    KLS[...] = jnp.zeros_like(KLS)

    def st_copy(th, k):
        return remote(
            STS.at[th], STR.at[th, me_v], st_s.at[th, k], st_r.at[th, k], (me_v + k) % nv, me_h
        )

    def stats(th):
        core_copy(1, th).wait_recv()
        y_copy(th).wait_recv()
        if th == 0:
            y_copy(0).wait_send()
            y_copy(1).start()
        own_t[th].wait()
        for k in range(1, nv):
            send_t(th, k).wait_recv()

        @pl.loop(0, nv)
        def _(i):
            r16 = pl.ds(pl.multiple_of(i * half, half), half)
            f = RY[th, r16, pl.ds(0, hv)]
            top = RY[th, r16, pl.ds(hv, 128)][:, 0:1]
            hi = jnp.floor(f * (1.0 / 4096.0) + 0.5)
            lo = f - hi * 4096.0
            both = jnp.concatenate([hi * (top / HI), lo * (top / LO)], axis=1)
            l = LG[th, r16] + RC[1, th, r16] + both
            LG[th, r16] = l
            t = T[th, i].astype(F32)
            m = jnp.max(l, axis=1, keepdims=True)
            mt = jnp.max(t, axis=1, keepdims=True)
            l, t = l - m, t - mt
            e = jnp.exp(l)
            cols = [
                m, jnp.sum(e, axis=1, keepdims=True), jnp.sum(e * (l - t), axis=1, keepdims=True),
                mt, jnp.sum(jnp.exp(t), axis=1, keepdims=True),
            ]
            block = jnp.zeros((half, rows), F32)
            for j, col in enumerate(cols):
                block = jnp.where(lane == j, col, block)
            TB[r16, :] = block

        flat = TB[...].T[0:8]
        STS[th] = flat
        STR[th, me_v] = flat
        for k in range(1, nv):
            st_copy(th, k).start()

    def g_copy(th, which):
        if which == 0:
            return remote(G.at[me_h, th], G.at[me_h, th], g_s.at[th, 0], g_r.at[th, 0], me_v, h_core)
        if which == 1:
            return remote(G.at[me_h, th], G.at[me_h, th], g_s.at[th, 1], g_r.at[th, 1], me_v, h_y)
        return remote(G.at[h_y, th], G.at[h_y, th], g_s.at[th, 2], g_r.at[th, 2], me_v, h_core)

    def grad(th):
        for k in range(1, nv):
            st_copy(th, k).wait_recv()
        p = [STR[th, d] for d in range(nv)]
        m_s, s_s, a, m_t, s_t = [[q[j : j + 1] for q in p] for j in range(5)]
        top_s, top_t = functools.reduce(jnp.maximum, m_s), functools.reduce(jnp.maximum, m_t)
        total_s = total_t = total_a = jnp.zeros_like(top_s)
        for d in range(nv):
            w = jnp.exp(m_s[d] - top_s)
            total_s = total_s + w * s_s[d]
            total_t = total_t + jnp.exp(m_t[d] - top_t) * s_t[d]
            total_a = total_a + w * (a[d] + s_s[d] * ((m_s[d] - top_s) - (m_t[d] - top_t)))
        log_s, log_t = jnp.log(total_s), jnp.log(total_t)
        kl = total_a / total_s - log_s + log_t
        KLS[th : th + 1, :] = kl
        TB[0:1, :] = top_s + log_s
        TB[1:2, :] = top_t + log_t
        TB[2:3, :] = kl
        TB[...] = TB[...].T

        @pl.loop(0, nv)
        def _(i):
            r16 = pl.ds(pl.multiple_of(i * half, half), half)
            b = TB[r16, :]
            u = LG[th, r16] - b[:, 0:1]
            gap = u - (T[th, i].astype(F32) - b[:, 1:2])
            G[me_h, th, r16] = (jnp.exp(u) * (gap - b[:, 2:3]) / tokens).astype(BF16)

        g_copy(th, 1).start()
        g_copy(th, 0).start()

    def kl_copy(k):
        return remote(KLS, KLR.at[me_h], kl_s.at[k], kl_r.at[k], me_v, (me_h + k) % nh)

    stats(0)
    grad(0)
    stats(1)
    grad(1)
    KLR[me_h] = KLS[...]
    for k in range(1, nh):
        kl_copy(k).start()

    def x_copy(s):
        return remote(GHS.at[s], GHR.at[s], x_s.at[s], x_r.at[s], 2 * z + 1 - x, me_h)

    def z_copy(s, k):
        to = (z + k) % nz
        return remote(ZS.at[s, to], ZR.at[s, z], z_s.at[s, k], z_r.at[s, k], 2 * to + x, me_h)

    def hidden_part(th):
        g_copy(th, 1).wait_recv()
        g_copy(th, 2).start()
        g_copy(th, 0).wait_recv()
        g_copy(th, 2).wait_recv()

        @pl.loop(0, ncb)
        def _(cb):
            s = th * ncb + cb
            r = lax.dot_general(
                G[:, th].reshape(nh * rows, vw), W[pl.ds(pl.multiple_of(cb * cw, cw), cw), :],
                (((1,), (1,)), ((), ())), preferred_element_type=F32,
            )
            RT[...] = r.reshape(nh, nz, 2, half, cw)
            GHS[s] = RT[:, :, 1 - x].astype(BF16)
            if th == 0:
                @pl.when(cb < 2)
                def _():
                    x_copy(s).start()
            GHK[s] = RT[:, :, x]

    def pass_on(s):
        x_copy(s).wait()

        @pl.when(s < 2 * ncb - 2)
        def _():
            x_copy(s + 2).start()

        for to in range(nz):
            ZS[s, to] = (GHK[s, :, to] + GHR[s, :, to].astype(F32)).astype(BF16)
        for k in range(1, nz):
            z_copy(s, k).start()

    tile = width // 8

    def gw_copy(i, slot):
        return pltpu.make_async_copy(
            GWS.at[slot], gw_o.at[pl.ds(pl.multiple_of(i * tile, tile), tile), :], gw_s.at[slot]
        )

    def weight_tile(i):
        slot = i % 2

        @pl.when(i >= 2)
        def _():
            gw_copy(i - 2, slot).wait()

        h = H[:, :, :, :, pl.ds(pl.multiple_of(i * tile, tile), tile)].reshape(2 * nh * rows, tile)

        @pl.loop(0, vw // nt)
        def _(j):
            cols = pl.ds(pl.multiple_of(j * nt, nt), nt)
            GWS[slot, :, cols] = lax.dot_general(
                h, G[:, :, :, cols].reshape(2 * nh * rows, nt),
                (((0,), (0,)), ((), ())), preferred_element_type=F32,
            ).astype(BF16)

        gw_copy(i, slot).start()

    hidden_part(0)
    pass_on(0)
    pass_on(1)
    hidden_part(1)

    @pl.loop(0, 8)
    def _(i):
        weight_tile(i)

        @pl.when(i < 2 * ncb - 2)
        def _():
            pass_on(i + 2)

    for i in (6, 7):
        gw_copy(i, i % 2).wait()
    for th in range(2):
        @pl.loop(0, ncb)
        def _(cb):
            s = th * ncb + cb
            total = ZS[s, z].astype(F32)
            for k in range(1, nz):
                z_copy(s, k).wait_recv()
                total = total + ZR[s, (z + nz - k) % nz].astype(F32)
            cols = pl.ds(pl.multiple_of(cb * cw, cw), cw)
            gh_o[:, pl.ds(th * half, half), cols] = total.astype(BF16)
            for k in range(1, nz):
                z_copy(s, k).wait_send()

    for k in range(1, nh):
        kl_copy(k).wait()
    kl_all = functools.reduce(jnp.add, [KLR[h] for h in range(nh)])
    kl_all = jnp.sum(jnp.sum(kl_all, axis=1, keepdims=True), axis=0, keepdims=True) / tokens
    loss_o[...] = kl_all
    y_copy(1).wait_send()
    for th in range(2):
        for kind in range(2):
            core_copy(kind, th).wait_send()
        for which in range(3):
            g_copy(th, which).wait_send()
        for k in range(1, nv):
            send_t(th, k).wait_send()
            st_copy(th, k).wait_send()


def hand_out(loss, gh, gw, loss_o, gh_o, gw_o, buf, buf_h, sem_in, sem_out):
    part = gw.shape[0] // 8
    blocks = [pl.ds(i * part, part) for i in range(8)]
    read = [pltpu.make_async_copy(gw.at[b], buf.at[b], sem_in.at[i]) for i, b in enumerate(blocks)]
    write = [pltpu.make_async_copy(buf.at[b], gw_o.at[b], sem_out.at[i]) for i, b in enumerate(blocks)]
    read.append(pltpu.make_async_copy(gh, buf_h, sem_in.at[8]))
    write.append(pltpu.make_async_copy(buf_h, gh_o, sem_out.at[8]))
    for copy in read:
        copy.start()
    loss_o[...] = loss[...]
    for copy, after in zip(read, write):
        copy.wait()
        after.start()
    for copy in write:
        copy.wait()


def fused_shards(student_hidden, head_weight, teacher_logits):
    nv, nh = lax.axis_size("vocab"), lax.axis_size("hid")
    tokens, width = student_hidden.shape
    vw = head_weight.shape[1]
    per = teacher_logits.shape[0]
    half, nz, ncb = per // 2, nv // 2, 4
    rows, cw, tile = nv * half, width // ncb, width // 8
    hidden = student_hidden.reshape(nv, nh, per, width)
    any_, vmem = pl.BlockSpec(memory_space=pl.ANY), pl.BlockSpec(memory_space=pltpu.VMEM)
    dma = lambda *shape: pltpu.SemaphoreType.DMA(shape)
    steps = 2 * ncb
    loss, gh, gw = pl.pallas_call(
        functools.partial(fused, tokens),
        out_shape=(
            jax.ShapeDtypeStruct((1, 1), F32),
            jax.ShapeDtypeStruct((nh, per, width), BF16),
            jax.ShapeDtypeStruct((width, vw), BF16),
        ),
        in_specs=[any_, any_, any_],
        out_specs=(vmem, vmem, any_),
        scratch_shapes=[
            pltpu.VMEM((width, vw), BF16),
            pltpu.VMEM((nh, 2, nv, half, width), BF16),
            pltpu.VMEM((2, nv, half, vw), BF16),
            pltpu.VMEM((2, 2, rows, vw), F32),
            pltpu.VMEM((2, 2, rows, vw), F32),
            pltpu.VMEM((2, rows, vw // 2 + 128), F32),
            pltpu.VMEM((2, rows, vw // 2 + 128), F32),
            pltpu.VMEM((2, rows, vw), F32),
            pltpu.VMEM((2, rows, vw), F32),
            pltpu.VMEM((2, 8, rows), F32),
            pltpu.VMEM((2, nv, 8, rows), F32),
            pltpu.VMEM((rows, rows), F32),
            pltpu.VMEM((8, rows), F32),
            pltpu.VMEM((nh, 8, rows), F32),
            pltpu.VMEM((nh, 2, rows, vw), BF16),
            pltpu.VMEM((nh, nz, 2, half, cw), F32),
            pltpu.VMEM((steps, nh, nz, half, cw), BF16),
            pltpu.VMEM((steps, nh, nz, half, cw), BF16),
            pltpu.VMEM((steps, nh, nz, half, cw), F32),
            pltpu.VMEM((steps, nz, nh, half, cw), BF16),
            pltpu.VMEM((steps, nz, nh, half, cw), BF16),
            pltpu.VMEM((2, tile, vw), BF16),
            dma(2 * nh + 2 + 4),
            dma(2, nv), dma(2, nv), dma(2, 2), dma(2, 2), dma(2), dma(2), dma(2, nv), dma(2, nv),
            dma(2, 3), dma(2, 3), dma(nh), dma(nh), dma(steps), dma(steps), dma(steps, nz), dma(steps, nz),
            dma(2),
        ],
        compiler_params=pltpu.CompilerParams(
            collective_id=0, has_side_effects=True, vmem_limit_bytes=60 * 1024 * 1024
        ),
        cost_estimate=pl.CostEstimate(
            flops=6 * tokens * width * vw, bytes_accessed=4 * width * vw, transcendentals=0
        ),
    )(hidden, head_weight, teacher_logits)
    loss, gh, gw = pl.pallas_call(
        hand_out,
        out_shape=tuple(jax.ShapeDtypeStruct(a.shape, a.dtype) for a in (loss, gh, gw)),
        in_specs=[vmem, any_, any_],
        out_specs=(vmem, any_, any_),
        scratch_shapes=[pltpu.VMEM(gw.shape, BF16), pltpu.VMEM(gh.shape, BF16), dma(9), dma(9)],
        compiler_params=pltpu.CompilerParams(vmem_limit_bytes=60 * 1024 * 1024),
        cost_estimate=pl.CostEstimate(flops=0, bytes_accessed=4 * width * vw, transcendentals=0),
    )(loss, gh, gw)
    return loss.reshape(()), gh.reshape(nh * per, width), gw


def shards(student_hidden, head_weight, teacher_logits):
    n_vocab = lax.axis_size("vocab")
    n_hid = lax.axis_size("hid")
    tokens, width = student_hidden.shape
    vocab_width = head_weight.shape[1]
    per_dev = teacher_logits.shape[0]
    mine = n_vocab * per_dev
    teacher = lax.all_to_all(
        teacher_logits, "vocab", split_axis=1, concat_axis=0, tiled=True
    ).astype(jnp.float32)
    hidden = student_hidden.reshape(n_vocab, n_hid, per_dev, width)
    hidden = hidden.transpose(1, 0, 2, 3).reshape(tokens, width)
    partial_value = jnp.dot(hidden, head_weight, preferred_element_type=jnp.float32)
    logits = lax.psum_scatter(partial_value, "hid", scatter_dimension=0, tiled=True)
    top_s = jnp.max(logits, axis=1, keepdims=True)
    top_t = jnp.max(teacher, axis=1, keepdims=True)
    e = jnp.exp(logits - top_s)
    stats = jnp.stack(
        [
            top_s[:, 0],
            jnp.sum(e, axis=1),
            jnp.sum(e * ((logits - top_s) - (teacher - top_t)), axis=1),
            top_t[:, 0],
            jnp.sum(jnp.exp(teacher - top_t), axis=1),
        ]
    )
    every = lax.all_gather(stats, "vocab", axis=0)
    m_s, s_s, a, m_t, s_t = [every[:, i] for i in range(5)]
    all_s, all_t = jnp.max(m_s, axis=0), jnp.max(m_t, axis=0)
    w = jnp.exp(m_s - all_s)
    total_s = jnp.sum(w * s_s, axis=0)
    total_t = jnp.sum(jnp.exp(m_t - all_t) * s_t, axis=0)
    log_s, log_t = jnp.log(total_s), jnp.log(total_t)
    gap = (m_s - all_s) - (m_t - all_t)
    kl_row = jnp.sum(w * (a + s_s * gap), axis=0) / total_s - log_s + log_t
    loss_value = lax.psum(jnp.sum(kl_row), "hid") / tokens
    student_log = logits - (all_s + log_s)[:, None]
    teacher_log = teacher - (all_t + log_t)[:, None]
    grad = (jnp.exp(student_log) * (student_log - teacher_log - kl_row[:, None]) / tokens).astype(
        jnp.bfloat16
    )
    grad = lax.all_gather(grad, "hid", axis=0, tiled=True)
    grad_hidden = lax.dot_general(
        grad, head_weight, (((1,), (1,)), ((), ())), preferred_element_type=jnp.float32
    ).astype(jnp.bfloat16)
    grad_hidden = grad_hidden.reshape(n_hid, n_vocab, per_dev, width).transpose(1, 0, 2, 3)
    grad_hidden = lax.psum_scatter(
        grad_hidden.reshape(tokens, width), "vocab", scatter_dimension=0, tiled=True
    )
    grad_weight = lax.dot_general(
        hidden, grad, (((0,), (0,)), ((), ())), preferred_element_type=jnp.float32
    ).astype(jnp.bfloat16)
    return (loss_value, grad_hidden, grad_weight)


def solution(mesh):
    fits = mesh.shape["hid"] == 4 and mesh.shape["vocab"] == 8
    def body(student_hidden, head_weight, teacher_logits):
        ok = fits and teacher_logits.shape[0] == 32
        return (fused_shards if ok else shards)(student_hidden, head_weight, teacher_logits)

    in_specs = (P(None, "hid"), P("hid", "vocab"), P(("vocab", "hid"), None))
    out_specs = (P(), P("vocab", "hid"), P("hid", "vocab"))
    return jax.shard_map(body, mesh=mesh, in_specs=in_specs, out_specs=out_specs, check_vma=False)
```

```python
import functools

import jax
import jax.numpy as jnp
from jax import lax
from jax.experimental import pallas as pl
from jax.experimental.pallas import tpu as pltpu
from jax.sharding import PartitionSpec as P


F32, BF16 = jnp.float32, jnp.bfloat16
HI, LO = 4095.0, 2047.0


def fused(
    tokens, hid, wgt, teach, loss_o, gh_o, gw_o,
    W, H, T, SC, RC, SY, RY, XF, LG, STS, STR, TB, KLS, KLR, G, RT, GHS, GHR, GHK, ZS, ZR, GWS,
    ld, t_s, t_r, c_s, c_r, y_s, y_r, st_s, st_r, g_s, g_r, kl_s, kl_r, x_s, x_r, z_s, z_r, gw_s,
):
    nz, nv = 2 * hid.shape[0], 4 * hid.shape[0]
    nh, per, width = hid.shape[3:]
    vw = wgt.shape[1]
    half = per // 2
    nq = H.shape[1]
    nb = nv // 2
    rows = nb * half
    ncb = GHS.shape[0] // nq
    cw = width // ncb
    nt = vw // 4
    hv = vw // 2
    me_v, me_h = lax.axis_index("vocab"), lax.axis_index("hid")
    y, c = me_h // 2, me_h % 2
    z, x = me_v // 2, me_v % 2
    h_core, h_y, h_far = 2 * y + 1 - c, 2 * (1 - y) + c, 2 * (1 - y) + 1 - c

    def remote(src, dst, send, recv, v, h):
        return pltpu.make_async_remote_copy(
            src_ref=src, dst_ref=dst, send_sem=send, recv_sem=recv,
            device_id={"vocab": v, "hid": h}, device_id_type=pl.DeviceIdType.MESH,
        )

    def load_h(k, q):
        h = (h_far, h_y, h_core, me_h)[k]
        return pltpu.make_async_copy(
            hid.at[:, q % 2, :, h, pl.ds(q // 2 * half, half), :], H.at[h, q], ld.at[nq * k + q]
        )

    def load_w(i):
        cols = pl.ds(pl.multiple_of(i * nt, nt), nt)
        return pltpu.make_async_copy(wgt.at[:, cols], W.at[:, cols], ld.at[nq * nh + 2 + i])

    for k in range(nh):
        for q in range(nq):
            load_h(k, q).start()
        if k == 0:
            for i in range(vw // nt):
                load_w(i).start()

    def teach_part(th, v):
        return teach.at[pl.ds(th * half, half), pl.ds(pl.multiple_of(v * vw, vw), vw)]

    own_t = [
        pltpu.make_async_copy(teach_part(th, me_v), T.at[2 * th + z % 2, z // 2 * 2 + x], ld.at[nq * nh + th]) for th in range(2)
    ]
    for copy in own_t:
        copy.start()

    barrier = pltpu.get_barrier_semaphore()
    for h in (h_core, h_y, h_far):
        pl.semaphore_signal(
            barrier, inc=1, device_id={"vocab": me_v, "hid": h}, device_id_type=pl.DeviceIdType.MESH
        )
    for k in range(1, nv):
        pl.semaphore_signal(
            barrier, inc=1, device_id={"vocab": (me_v + k) % nv, "hid": me_h},
            device_id_type=pl.DeviceIdType.MESH,
        )
    pl.semaphore_wait(barrier, nh - 1 + nv - 1)

    def send_t(th, k):
        v = (me_v + k) % nv
        return remote(teach_part(th, v), T.at[2 * th + z % 2, z // 2 * 2 + x], t_s.at[th, k], t_r.at[th, k], v, me_h)

    for k in range(1, nv):
        send_t(0, k).start()

    def project(k, out):
        h = (h_far, h_y, h_core, me_h)[k]
        for q in range(nq):
            load_h(k, q).wait()

        @pl.loop(0, vw // nt)
        def _(i):
            if k == 0:
                load_w(i).wait()
            cols = pl.ds(pl.multiple_of(i * nt, nt), nt)
            r = jnp.dot(H[h].reshape(nq * rows, width), W[:, cols], preferred_element_type=F32)
            out[:, :, cols] = r.reshape(nq, rows, nt)

    def core_copy(kind, th):
        return remote(
            SC.at[kind, th], RC.at[kind, th], c_s.at[kind, th], c_r.at[kind, th], me_v, h_core
        )

    def y_copy(th):
        return remote(SY.at[th], RY.at[th], y_s.at[th], y_r.at[th], me_v, h_y)

    project(0, SC.at[0])
    for th in range(nq):
        core_copy(0, th).start()
    project(1, XF)
    for th in range(nq):
        core_copy(0, th).wait_recv()

        @pl.loop(0, nb)
        def _(i):
            r16 = pl.ds(pl.multiple_of(i * half, half), half)
            s = XF[th, r16] + RC[0, th, r16]
            top = jnp.maximum(jnp.max(jnp.abs(s), axis=1, keepdims=True), 1e-20)
            hi = jnp.floor(s[:, :hv] * (HI / top) + 0.5)
            lo = jnp.floor(s[:, hv:] * (LO / top) + 0.5)
            SY[th, r16, pl.ds(0, hv)] = hi * 4096.0 + lo
            SY[th, r16, pl.ds(hv, 128)] = jnp.broadcast_to(top, (half, 128))

        if th < 2:
            y_copy(th).start()
    project(2, SC.at[1])
    for th in range(nq):
        core_copy(1, th).start()
    project(3, LG)
    for k in range(1, nv):
        send_t(1, k).start()

    lane = lax.broadcasted_iota(jnp.int32, (half, 128), 1)
    live = lax.broadcasted_iota(jnp.int32, (1, 128), 1) < rows
    KLS[...] = jnp.zeros_like(KLS)
    TB[...] = jnp.zeros_like(TB)

    def st_copy(th, k):
        return remote(
            STS.at[th], STR.at[th, me_v], st_s.at[th, k], st_r.at[th, k], (me_v + k) % nv, me_h
        )

    def stats(th):
        core_copy(1, th).wait_recv()
        y_copy(th).wait_recv()
        y_copy(th).wait_send()
        if th + 2 < nq:
            y_copy(th + 2).start()
        if th % 2 == 0:
            own_t[th // 2].wait()
            for k in range(1, nv):
                send_t(th // 2, k).wait_recv()

        @pl.loop(0, nb)
        def _(i):
            r16 = pl.ds(pl.multiple_of(i * half, half), half)
            f = RY[th, r16, pl.ds(0, hv)]
            top = RY[th, r16, pl.ds(hv, 128)][:, 0:1]
            hi = jnp.floor(f * (1.0 / 4096.0) + 0.5)
            lo = f - hi * 4096.0
            both = jnp.concatenate([hi * (top / HI), lo * (top / LO)], axis=1)
            l = LG[th, r16] + RC[1, th, r16] + both
            LG[th, r16] = l
            t = T[th, i].astype(F32)
            m = jnp.max(l, axis=1, keepdims=True)
            mt = jnp.max(t, axis=1, keepdims=True)
            l, t = l - m, t - mt
            e = jnp.exp(l)
            cols = [
                m, jnp.sum(e, axis=1, keepdims=True), jnp.sum(e * (l - t), axis=1, keepdims=True),
                mt, jnp.sum(jnp.exp(t), axis=1, keepdims=True),
            ]
            block = jnp.zeros((half, 128), F32)
            for j, col in enumerate(cols):
                block = jnp.where(lane == j, col, block)
            TB[r16, :] = block

        flat = TB[...].T[0:8]
        STS[th] = flat
        STR[th, me_v] = flat
        for k in range(1, nv):
            st_copy(th, k).start()

    def g_copy(th, which):
        if which == 0:
            return remote(G.at[me_h, th], G.at[me_h, th], g_s.at[th, 0], g_r.at[th, 0], me_v, h_core)
        if which == 1:
            return remote(G.at[me_h, th], G.at[me_h, th], g_s.at[th, 1], g_r.at[th, 1], me_v, h_y)
        return remote(G.at[h_y, th], G.at[h_y, th], g_s.at[th, 2], g_r.at[th, 2], me_v, h_core)

    def grad(th):
        for k in range(1, nv):
            st_copy(th, k).wait_recv()
        p = [STR[th, d] for d in range(nv)]
        m_s, s_s, a, m_t, s_t = [[q[j : j + 1] for q in p] for j in range(5)]
        top_s, top_t = functools.reduce(jnp.maximum, m_s), functools.reduce(jnp.maximum, m_t)
        total_s = total_t = total_a = jnp.zeros_like(top_s)
        for d in range(nv):
            w = jnp.exp(m_s[d] - top_s)
            total_s = total_s + w * s_s[d]
            total_t = total_t + jnp.exp(m_t[d] - top_t) * s_t[d]
            total_a = total_a + w * (a[d] + s_s[d] * ((m_s[d] - top_s) - (m_t[d] - top_t)))
        log_s, log_t = jnp.log(total_s), jnp.log(total_t)
        kl = jnp.where(live, total_a / total_s - log_s + log_t, 0.0)
        KLS[th : th + 1, :] = kl
        TB[0:1, :] = jnp.where(live, top_s + log_s, 0.0)
        TB[1:2, :] = jnp.where(live, top_t + log_t, 0.0)
        TB[2:3, :] = kl
        TB[...] = TB[...].T

        @pl.loop(0, nb)
        def _(i):
            r16 = pl.ds(pl.multiple_of(i * half, half), half)
            b = TB[r16, :]
            u = LG[th, r16] - b[:, 0:1]
            gap = u - (T[th, i].astype(F32) - b[:, 1:2])
            G[me_h, th, r16] = (jnp.exp(u) * (gap - b[:, 2:3]) / tokens).astype(BF16)

        g_copy(th, 1).start()
        g_copy(th, 0).start()

    def kl_copy(k):
        return remote(KLS, KLR.at[me_h], kl_s.at[k], kl_r.at[k], me_v, (me_h + k) % nh)

    def x_copy(s):
        return remote(GHS.at[s], GHR.at[s], x_s.at[s], x_r.at[s], 2 * z + 1 - x, me_h)

    def zp_of(s):
        return s // ncb % 2

    def z_copy(s, d, k):
        return remote(
            ZS.at[s, d], ZR.at[s, k], z_s.at[s, d], z_r.at[s, k], 2 * (zp_of(s) + 2 * d) + x, me_h
        )

    def z_sends(s, act):
        for d in range(2):
            for k in range(1, nz):
                @pl.when((zp_of(s) + 2 * d + k) % nz == z)
                def _():
                    act(z_copy(s, d, k))

    def hidden_part(th):
        g_copy(th, 1).wait_recv()
        g_copy(th, 2).start()
        g_copy(th, 0).wait_recv()
        g_copy(th, 2).wait_recv()

        @pl.loop(0, ncb)
        def _(cb):
            s = th * ncb + cb
            r = lax.dot_general(
                G[:, th].reshape(nh * rows, vw), W[pl.ds(pl.multiple_of(cb * cw, cw), cw), :],
                (((1,), (1,)), ((), ())), preferred_element_type=F32,
            )
            RT[...] = r.reshape(nh, 2, 2, half, cw)
            GHS[s] = RT[:, :, 1 - x].astype(BF16)
            x_copy(s).start()
            GHK[s] = RT[:, :, x]

    def pass_on(s):
        x_copy(s).wait()
        for d in range(2):
            ZS[s, d] = (GHK[s, :, d] + GHR[s, :, d].astype(F32)).astype(BF16)
        z_sends(s, lambda copy: copy.start())

    tile = width // 8

    def gw_copy(i, slot):
        return pltpu.make_async_copy(
            GWS.at[slot], gw_o.at[pl.ds(pl.multiple_of(i * tile, tile), tile), :], gw_s.at[slot]
        )

    def weight_tile(i):
        slot = i % 2

        @pl.when(i >= 2)
        def _():
            gw_copy(i - 2, slot).wait()

        h = H[:, :, :, :, :, pl.ds(pl.multiple_of(i * tile, tile), tile)].reshape(nq * nh * rows, tile)

        @pl.loop(0, vw // nt)
        def _(j):
            cols = pl.ds(pl.multiple_of(j * nt, nt), nt)
            GWS[slot, :, cols] = lax.dot_general(
                h, G[:, :, :, cols].reshape(nq * nh * rows, nt),
                (((0,), (0,)), ((), ())), preferred_element_type=F32,
            ).astype(BF16)

        gw_copy(i, slot).start()

    for q in range(3):
        stats(q)
        grad(q)
    hidden_part(0)
    stats(3)
    grad(3)
    KLR[me_h] = KLS[...]
    for k in range(1, nh):
        kl_copy(k).start()
    hidden_part(1)
    pass_on(0)
    hidden_part(2)
    pass_on(1)
    pass_on(2)
    hidden_part(3)
    pass_on(3)

    @pl.loop(0, 8)
    def _(i):
        weight_tile(i)

        @pl.when(i < 4)
        def _():
            pass_on(i + 4)

    for i in (6, 7):
        gw_copy(i, i % 2).wait()
    for q in range(nq):
        @pl.when(z % 2 == q % 2)
        def _():
            for cb in range(ncb):
                s = q * ncb + cb
                total = ZS[s, z // 2].astype(F32)
                for k in range(1, nz):
                    pltpu.make_async_copy(ZR.at[s, k], ZR.at[s, k], z_r.at[s, k]).wait()
                    total = total + ZR[s, k].astype(F32)
                gh_o[:, pl.ds(q // 2 * half, half), pl.ds(cb * cw, cw)] = total.astype(BF16)

    for s in range(nq * ncb):
        z_sends(s, lambda copy: copy.wait_send())
    for k in range(1, nh):
        kl_copy(k).wait()
    kl_all = functools.reduce(jnp.add, [KLR[h] for h in range(nh)])
    kl_all = jnp.sum(jnp.sum(kl_all, axis=1, keepdims=True), axis=0, keepdims=True) / tokens
    loss_o[...] = kl_all
    for th in range(nq):
        for kind in range(2):
            core_copy(kind, th).wait_send()
        for which in range(3):
            g_copy(th, which).wait_send()
        for k in range(1, nv):
            st_copy(th, k).wait_send()
    for th in range(2):
        for k in range(1, nv):
            send_t(th, k).wait_send()


def hand_out(loss, gh, gw, loss_o, gh_o, gw_o, buf, buf_h, sem_in, sem_out):
    part = gw.shape[0] // 8
    blocks = [pl.ds(i * part, part) for i in range(8)]
    read = [pltpu.make_async_copy(gw.at[b], buf.at[b], sem_in.at[i]) for i, b in enumerate(blocks)]
    write = [pltpu.make_async_copy(buf.at[b], gw_o.at[b], sem_out.at[i]) for i, b in enumerate(blocks)]
    read.append(pltpu.make_async_copy(gh, buf_h, sem_in.at[8]))
    write.append(pltpu.make_async_copy(buf_h, gh_o, sem_out.at[8]))
    for copy in read:
        copy.start()
    loss_o[...] = loss[...]
    for copy, after in zip(read, write):
        copy.wait()
        after.start()
    for copy in write:
        copy.wait()


def fused_shards(student_hidden, head_weight, teacher_logits):
    nv, nh = lax.axis_size("vocab"), lax.axis_size("hid")
    tokens, width = student_hidden.shape
    vw = head_weight.shape[1]
    per = teacher_logits.shape[0]
    half, nz, nq, ncb = per // 2, nv // 2, 4, 2
    nb = nv // 2
    rows, cw, tile = nb * half, width // ncb, width // 8
    hidden = student_hidden.reshape(nz // 2, 2, 2, nh, per, width)
    any_, vmem = pl.BlockSpec(memory_space=pl.ANY), pl.BlockSpec(memory_space=pltpu.VMEM)
    dma = lambda *shape: pltpu.SemaphoreType.DMA(shape)
    steps = nq * ncb
    loss, gh, gw = pl.pallas_call(
        functools.partial(fused, tokens),
        out_shape=(
            jax.ShapeDtypeStruct((1, 1), F32),
            jax.ShapeDtypeStruct((nh, per, width), BF16),
            jax.ShapeDtypeStruct((width, vw), BF16),
        ),
        in_specs=[any_, any_, any_],
        out_specs=(vmem, vmem, any_),
        scratch_shapes=[
            pltpu.VMEM((width, vw), BF16),
            pltpu.VMEM((nh, nq, 2, 2, half, width), BF16),
            pltpu.VMEM((nq, nb, half, vw), BF16),
            pltpu.VMEM((2, nq, rows, vw), F32),
            pltpu.VMEM((2, nq, rows, vw), F32),
            pltpu.VMEM((nq, rows, vw // 2 + 128), F32),
            pltpu.VMEM((nq, rows, vw // 2 + 128), F32),
            pltpu.VMEM((nq, rows, vw), F32),
            pltpu.VMEM((nq, rows, vw), F32),
            pltpu.VMEM((nq, 8, 128), F32),
            pltpu.VMEM((nq, nv, 8, 128), F32),
            pltpu.VMEM((128, 128), F32),
            pltpu.VMEM((8, 128), F32),
            pltpu.VMEM((nh, 8, 128), F32),
            pltpu.VMEM((nh, nq, rows, vw), BF16),
            pltpu.VMEM((nh, 2, 2, half, cw), F32),
            pltpu.VMEM((steps, nh, 2, half, cw), BF16),
            pltpu.VMEM((steps, nh, 2, half, cw), BF16),
            pltpu.VMEM((steps, nh, 2, half, cw), F32),
            pltpu.VMEM((steps, 2, nh, half, cw), BF16),
            pltpu.VMEM((steps, nz, nh, half, cw), BF16),
            pltpu.VMEM((2, tile, vw), BF16),
            dma(nq * nh + 2 + 4),
            dma(2, nv), dma(2, nv), dma(2, nq), dma(2, nq), dma(nq), dma(nq), dma(nq, nv), dma(nq, nv),
            dma(nq, 3), dma(nq, 3), dma(nh), dma(nh), dma(steps), dma(steps), dma(steps, 2), dma(steps, nz),
            dma(2),
        ],
        compiler_params=pltpu.CompilerParams(
            collective_id=0, has_side_effects=True, vmem_limit_bytes=60 * 1024 * 1024
        ),
        cost_estimate=pl.CostEstimate(
            flops=6 * tokens * width * vw, bytes_accessed=4 * width * vw, transcendentals=0
        ),
    )(hidden, head_weight, teacher_logits)
    loss, gh, gw = pl.pallas_call(
        hand_out,
        out_shape=tuple(jax.ShapeDtypeStruct(a.shape, a.dtype) for a in (loss, gh, gw)),
        in_specs=[vmem, any_, any_],
        out_specs=(vmem, any_, any_),
        scratch_shapes=[pltpu.VMEM(gw.shape, BF16), pltpu.VMEM(gh.shape, BF16), dma(9), dma(9)],
        compiler_params=pltpu.CompilerParams(vmem_limit_bytes=60 * 1024 * 1024),
        cost_estimate=pl.CostEstimate(flops=0, bytes_accessed=4 * width * vw, transcendentals=0),
    )(loss, gh, gw)
    return loss.reshape(()), gh.reshape(nh * per, width), gw


def shards(student_hidden, head_weight, teacher_logits):
    n_vocab = lax.axis_size("vocab")
    n_hid = lax.axis_size("hid")
    tokens, width = student_hidden.shape
    vocab_width = head_weight.shape[1]
    per_dev = teacher_logits.shape[0]
    mine = n_vocab * per_dev
    teacher = lax.all_to_all(
        teacher_logits, "vocab", split_axis=1, concat_axis=0, tiled=True
    ).astype(jnp.float32)
    hidden = student_hidden.reshape(n_vocab, n_hid, per_dev, width)
    hidden = hidden.transpose(1, 0, 2, 3).reshape(tokens, width)
    partial_value = jnp.dot(hidden, head_weight, preferred_element_type=jnp.float32)
    logits = lax.psum_scatter(partial_value, "hid", scatter_dimension=0, tiled=True)
    top_s = jnp.max(logits, axis=1, keepdims=True)
    top_t = jnp.max(teacher, axis=1, keepdims=True)
    e = jnp.exp(logits - top_s)
    stats = jnp.stack(
        [
            top_s[:, 0],
            jnp.sum(e, axis=1),
            jnp.sum(e * ((logits - top_s) - (teacher - top_t)), axis=1),
            top_t[:, 0],
            jnp.sum(jnp.exp(teacher - top_t), axis=1),
        ]
    )
    every = lax.all_gather(stats, "vocab", axis=0)
    m_s, s_s, a, m_t, s_t = [every[:, i] for i in range(5)]
    all_s, all_t = jnp.max(m_s, axis=0), jnp.max(m_t, axis=0)
    w = jnp.exp(m_s - all_s)
    total_s = jnp.sum(w * s_s, axis=0)
    total_t = jnp.sum(jnp.exp(m_t - all_t) * s_t, axis=0)
    log_s, log_t = jnp.log(total_s), jnp.log(total_t)
    gap = (m_s - all_s) - (m_t - all_t)
    kl_row = jnp.sum(w * (a + s_s * gap), axis=0) / total_s - log_s + log_t
    loss_value = lax.psum(jnp.sum(kl_row), "hid") / tokens
    student_log = logits - (all_s + log_s)[:, None]
    teacher_log = teacher - (all_t + log_t)[:, None]
    grad = (jnp.exp(student_log) * (student_log - teacher_log - kl_row[:, None]) / tokens).astype(
        jnp.bfloat16
    )
    grad = lax.all_gather(grad, "hid", axis=0, tiled=True)
    grad_hidden = lax.dot_general(
        grad, head_weight, (((1,), (1,)), ((), ())), preferred_element_type=jnp.float32
    ).astype(jnp.bfloat16)
    grad_hidden = grad_hidden.reshape(n_hid, n_vocab, per_dev, width).transpose(1, 0, 2, 3)
    grad_hidden = lax.psum_scatter(
        grad_hidden.reshape(tokens, width), "vocab", scatter_dimension=0, tiled=True
    )
    grad_weight = lax.dot_general(
        hidden, grad, (((0,), (0,)), ((), ())), preferred_element_type=jnp.float32
    ).astype(jnp.bfloat16)
    return (loss_value, grad_hidden, grad_weight)


def solution(mesh):
    fits = mesh.shape["hid"] == 4 and mesh.shape["vocab"] == 8
    def body(student_hidden, head_weight, teacher_logits):
        ok = fits and teacher_logits.shape[0] == 32
        return (fused_shards if ok else shards)(student_hidden, head_weight, teacher_logits)

    in_specs = (P(None, "hid"), P("hid", "vocab"), P(("vocab", "hid"), None))
    out_specs = (P(), P("vocab", "hid"), P("hid", "vocab"))
    return jax.shard_map(body, mesh=mesh, in_specs=in_specs, out_specs=out_specs, check_vma=False)
```

```python
import functools

import jax
import jax.numpy as jnp
from jax import lax
from jax.experimental import pallas as pl
from jax.experimental.pallas import tpu as pltpu
from jax.sharding import PartitionSpec as P


F32, BF16 = jnp.float32, jnp.bfloat16
HI, LO = 4095.0, 2047.0


def fused(
    tokens, hid, wgt, teach, loss_o, gh_o, gw_o,
    W, H, T, SC, RC, SY, RY, XF, LG, STS, STR, TB, KLS, KLR, G, RT, GHS, GHR, GHK, ZS, ZR, GWS, HT,
    ld, t_s, t_r, c_s, c_r, y_s, y_r, st_s, st_r, g_s, g_r, kl_s, kl_r, x_s, x_r, z_s, z_r, gw_s,
):
    nz, nv = 2 * hid.shape[0], 4 * hid.shape[0]
    nh, per, width = hid.shape[3:]
    vw = wgt.shape[1]
    half = per // 2
    nq = H.shape[1]
    nb = nv // 2
    rows = nb * half
    ncb = GHS.shape[0] // nq
    cw = width // ncb
    nt = vw // 4
    hv = vw // 2
    me_v, me_h = lax.axis_index("vocab"), lax.axis_index("hid")
    y, c = me_h // 2, me_h % 2
    z, x = me_v // 2, me_v % 2
    h_core, h_y, h_far = 2 * y + 1 - c, 2 * (1 - y) + c, 2 * (1 - y) + 1 - c

    def remote(src, dst, send, recv, v, h):
        return pltpu.make_async_remote_copy(
            src_ref=src, dst_ref=dst, send_sem=send, recv_sem=recv,
            device_id={"vocab": v, "hid": h}, device_id_type=pl.DeviceIdType.MESH,
        )

    def load_h(k, q):
        h = (h_far, h_y, h_core, me_h)[k]
        return pltpu.make_async_copy(
            hid.at[:, q % 2, :, h, pl.ds(q // 2 * half, half), :], H.at[h, q], ld.at[nq * k + q]
        )

    def load_w(i):
        cols = pl.ds(pl.multiple_of(i * nt, nt), nt)
        return pltpu.make_async_copy(wgt.at[:, cols], W.at[:, cols], ld.at[nq * nh + 2 + i])

    for k in range(nh):
        for q in range(nq):
            load_h(k, q).start()
        if k == 0:
            for i in range(vw // nt):
                load_w(i).start()

    def teach_part(th, v):
        return teach.at[pl.ds(th * half, half), pl.ds(pl.multiple_of(v * vw, vw), vw)]

    own_t = [
        pltpu.make_async_copy(teach_part(th, me_v), T.at[2 * th + z % 2, z // 2 * 2 + x], ld.at[nq * nh + th]) for th in range(2)
    ]
    for copy in own_t:
        copy.start()

    barrier = pltpu.get_barrier_semaphore()
    for h in (h_core, h_y, h_far):
        pl.semaphore_signal(
            barrier, inc=1, device_id={"vocab": me_v, "hid": h}, device_id_type=pl.DeviceIdType.MESH
        )
    for k in range(1, nv):
        pl.semaphore_signal(
            barrier, inc=1, device_id={"vocab": (me_v + k) % nv, "hid": me_h},
            device_id_type=pl.DeviceIdType.MESH,
        )
    pl.semaphore_wait(barrier, nh - 1 + nv - 1)

    def send_t(th, k):
        v = (me_v + k) % nv
        return remote(teach_part(th, v), T.at[2 * th + z % 2, z // 2 * 2 + x], t_s.at[th, k], t_r.at[th, k], v, me_h)

    for k in range(1, nv):
        send_t(0, k).start()

    def project(k, out):
        h = (h_far, h_y, h_core, me_h)[k]
        for q in range(nq):
            load_h(k, q).wait()

        @pl.loop(0, vw // nt)
        def _(i):
            if k == 0:
                load_w(i).wait()
            cols = pl.ds(pl.multiple_of(i * nt, nt), nt)
            r = jnp.dot(H[h].reshape(nq * rows, width), W[:, cols], preferred_element_type=F32)
            out[:, :, cols] = r.reshape(nq, rows, nt)

    def core_copy(kind, th):
        return remote(
            SC.at[kind, th], RC.at[kind, th], c_s.at[kind, th], c_r.at[kind, th], me_v, h_core
        )

    def y_copy(th):
        return remote(SY.at[th], RY.at[th], y_s.at[th], y_r.at[th], me_v, h_y)

    project(0, SC.at[0])
    for th in range(nq):
        core_copy(0, th).start()
    project(1, XF)
    for th in range(nq):
        core_copy(0, th).wait_recv()

        @pl.loop(0, nb)
        def _(i):
            r16 = pl.ds(pl.multiple_of(i * half, half), half)
            s = XF[th, r16] + RC[0, th, r16]
            top = jnp.maximum(jnp.max(jnp.abs(s), axis=1, keepdims=True), 1e-20)
            hi = jnp.floor(s[:, :hv] * (HI / top) + 0.5)
            lo = jnp.floor(s[:, hv:] * (LO / top) + 0.5)
            SY[th, r16, pl.ds(0, hv)] = hi * 4096.0 + lo
            SY[th, r16, pl.ds(hv, 128)] = jnp.broadcast_to(top, (half, 128))

        if th < 2:
            y_copy(th).start()
    for k in (2, 3):
        for q in range(nq):
            load_h(k, q).wait()

    @pl.loop(0, vw // nt)
    def _(i):
        cols = pl.ds(pl.multiple_of(i * nt, nt), nt)
        r = jnp.dot(
            H[pl.ds(2 * y, 2)].reshape(2 * nq * rows, width), W[:, cols], preferred_element_type=F32
        )
        r = r.reshape(2, nq, rows, nt)
        first = c == 0
        SC[1, :, :, cols] = jnp.where(first, r[1], r[0])
        LG[:, :, cols] = jnp.where(first, r[0], r[1])

    for th in range(nq):
        core_copy(1, th).start()
    for k in range(1, nv):
        send_t(1, k).start()

    @pl.loop(0, width // 256)
    def _(i):
        d = pl.ds(pl.multiple_of(i * 256, 256), 256)
        HT[d, :] = H[:, :, :, :, :, d].reshape(nh * nq * rows, 256).T


    lane = lax.broadcasted_iota(jnp.int32, (half, 128), 1)
    live = lax.broadcasted_iota(jnp.int32, (1, 128), 1) < rows
    KLS[...] = jnp.zeros_like(KLS)
    TB[...] = jnp.zeros_like(TB)

    def st_copy(th, k):
        return remote(
            STS.at[th], STR.at[th, me_v], st_s.at[th, k], st_r.at[th, k], (me_v + k) % nv, me_h
        )

    def stats(th):
        core_copy(1, th).wait_recv()
        y_copy(th).wait_recv()
        y_copy(th).wait_send()
        if th + 2 < nq:
            y_copy(th + 2).start()
        if th % 2 == 0:
            own_t[th // 2].wait()
            for k in range(1, nv):
                send_t(th // 2, k).wait_recv()

        @pl.loop(0, nb)
        def _(i):
            r16 = pl.ds(pl.multiple_of(i * half, half), half)
            f = RY[th, r16, pl.ds(0, hv)]
            top = RY[th, r16, pl.ds(hv, 128)][:, 0:1]
            hi = jnp.floor(f * (1.0 / 4096.0) + 0.5)
            lo = f - hi * 4096.0
            both = jnp.concatenate([hi * (top / HI), lo * (top / LO)], axis=1)
            l = LG[th, r16] + RC[1, th, r16] + both
            LG[th, r16] = l
            t = T[th, i].astype(F32)
            m = jnp.max(l, axis=1, keepdims=True)
            mt = jnp.max(t, axis=1, keepdims=True)
            l, t = l - m, t - mt
            e = jnp.exp(l)
            cols = [
                m, jnp.sum(e, axis=1, keepdims=True), jnp.sum(e * (l - t), axis=1, keepdims=True),
                mt, jnp.sum(jnp.exp(t), axis=1, keepdims=True),
            ]
            block = jnp.zeros((half, 128), F32)
            for j, col in enumerate(cols):
                block = jnp.where(lane == j, col, block)
            TB[r16, :] = block

        flat = TB[...].T[0:8]
        STS[th] = flat
        STR[th, me_v] = flat
        for k in range(1, nv):
            st_copy(th, k).start()

    def g_copy(th, which):
        if which == 0:
            return remote(G.at[me_h, th], G.at[me_h, th], g_s.at[th, 0], g_r.at[th, 0], me_v, h_core)
        if which == 1:
            return remote(G.at[me_h, th], G.at[me_h, th], g_s.at[th, 1], g_r.at[th, 1], me_v, h_y)
        return remote(G.at[h_y, th], G.at[h_y, th], g_s.at[th, 2], g_r.at[th, 2], me_v, h_core)

    def grad(th):
        for k in range(1, nv):
            st_copy(th, k).wait_recv()
        p = [STR[th, d] for d in range(nv)]
        m_s, s_s, a, m_t, s_t = [[q[j : j + 1] for q in p] for j in range(5)]
        top_s, top_t = functools.reduce(jnp.maximum, m_s), functools.reduce(jnp.maximum, m_t)
        total_s = total_t = total_a = jnp.zeros_like(top_s)
        for d in range(nv):
            w = jnp.exp(m_s[d] - top_s)
            total_s = total_s + w * s_s[d]
            total_t = total_t + jnp.exp(m_t[d] - top_t) * s_t[d]
            total_a = total_a + w * (a[d] + s_s[d] * ((m_s[d] - top_s) - (m_t[d] - top_t)))
        log_s, log_t = jnp.log(total_s), jnp.log(total_t)
        kl = jnp.where(live, total_a / total_s - log_s + log_t, 0.0)
        KLS[th : th + 1, :] = kl
        TB[0:1, :] = jnp.where(live, top_s + log_s, 0.0)
        TB[1:2, :] = jnp.where(live, top_t + log_t, 0.0)
        TB[2:3, :] = kl
        TB[...] = TB[...].T

        @pl.loop(0, nb)
        def _(i):
            r16 = pl.ds(pl.multiple_of(i * half, half), half)
            b = TB[r16, :]
            u = LG[th, r16] - b[:, 0:1]
            gap = u - (T[th, i].astype(F32) - b[:, 1:2])
            G[me_h, th, r16] = (jnp.exp(u) * (gap - b[:, 2:3]) / tokens).astype(BF16)

        g_copy(th, 1).start()
        g_copy(th, 0).start()

    def kl_copy(k):
        return remote(KLS, KLR.at[me_h], kl_s.at[k], kl_r.at[k], me_v, (me_h + k) % nh)

    def x_copy(s):
        return remote(GHS.at[s], GHR.at[s], x_s.at[s], x_r.at[s], 2 * z + 1 - x, me_h)

    def zp_of(s):
        return s // ncb % 2

    def z_copy(s, d, k):
        return remote(
            ZS.at[s, d], ZR.at[s, k], z_s.at[s, d], z_r.at[s, k], 2 * (zp_of(s) + 2 * d) + x, me_h
        )

    def z_sends(s, act):
        for d in range(2):
            for k in range(1, nz):
                @pl.when((zp_of(s) + 2 * d + k) % nz == z)
                def _():
                    act(z_copy(s, d, k))

    def hidden_part(th):
        g_copy(th, 1).wait_recv()
        g_copy(th, 2).start()
        g_copy(th, 0).wait_recv()
        g_copy(th, 2).wait_recv()

        @pl.loop(0, ncb)
        def _(cb):
            s = th * ncb + cb
            r = lax.dot_general(
                G[:, th].reshape(nh * rows, vw), W[pl.ds(pl.multiple_of(cb * cw, cw), cw), :],
                (((1,), (1,)), ((), ())), preferred_element_type=F32,
            )
            RT[...] = r.reshape(nh, 2, 2, half, cw)
            GHS[s] = RT[:, :, 1 - x].astype(BF16)
            x_copy(s).start()
            GHK[s] = RT[:, :, x]

    def pass_on(s):
        x_copy(s).wait()
        for d in range(2):
            ZS[s, d] = (GHK[s, :, d] + GHR[s, :, d].astype(F32)).astype(BF16)
        z_sends(s, lambda copy: copy.start())

    tile = width // 4

    def gw_copy(i, slot):
        return pltpu.make_async_copy(
            GWS.at[slot], gw_o.at[pl.ds(pl.multiple_of(i * tile, tile), tile), :], gw_s.at[slot]
        )

    def weight_tile(i):
        slot = i % 2

        @pl.when(i >= 2)
        def _():
            gw_copy(i - 2, slot).wait()

        h = pl.ds(pl.multiple_of(i * tile, tile), tile)

        @pl.loop(0, vw // nt)
        def _(j):
            cols = pl.ds(pl.multiple_of(j * nt, nt), nt)
            GWS[slot, :, cols] = lax.dot_general(
                HT[h, :], G[:, :, :, cols].reshape(nq * nh * rows, nt),
                (((1,), (0,)), ((), ())), preferred_element_type=F32,
            ).astype(BF16)

        gw_copy(i, slot).start()

    for q in range(3):
        stats(q)
        grad(q)
    hidden_part(0)
    stats(3)
    grad(3)
    KLR[me_h] = KLS[...]
    for k in range(1, nh):
        kl_copy(k).start()
    hidden_part(1)
    pass_on(0)
    hidden_part(2)
    pass_on(1)
    pass_on(2)
    hidden_part(3)
    pass_on(3)

    @pl.loop(0, 4)
    def _(i):
        weight_tile(i)
        pass_on(i + 4)

    for i in (2, 3):
        gw_copy(i, i % 2).wait()
    for q in range(nq):
        @pl.when(z % 2 == q % 2)
        def _():
            for cb in range(ncb):
                s = q * ncb + cb
                total = ZS[s, z // 2].astype(F32)
                for k in range(1, nz):
                    pltpu.make_async_copy(ZR.at[s, k], ZR.at[s, k], z_r.at[s, k]).wait()
                    total = total + ZR[s, k].astype(F32)
                gh_o[:, pl.ds(q // 2 * half, half), pl.ds(cb * cw, cw)] = total.astype(BF16)

    for s in range(nq * ncb):
        z_sends(s, lambda copy: copy.wait_send())
    for k in range(1, nh):
        kl_copy(k).wait()
    kl_all = functools.reduce(jnp.add, [KLR[h] for h in range(nh)])
    kl_all = jnp.sum(jnp.sum(kl_all, axis=1, keepdims=True), axis=0, keepdims=True) / tokens
    loss_o[...] = kl_all
    for th in range(nq):
        for kind in range(2):
            core_copy(kind, th).wait_send()
        for which in range(3):
            g_copy(th, which).wait_send()
        for k in range(1, nv):
            st_copy(th, k).wait_send()
    for th in range(2):
        for k in range(1, nv):
            send_t(th, k).wait_send()


def hand_out(loss, gh, gw, loss_o, gh_o, gw_o, buf, buf_h, sem_in, sem_out):
    part = gw.shape[0] // 8
    blocks = [pl.ds(i * part, part) for i in range(8)]
    read = [pltpu.make_async_copy(gw.at[b], buf.at[b], sem_in.at[i]) for i, b in enumerate(blocks)]
    write = [pltpu.make_async_copy(buf.at[b], gw_o.at[b], sem_out.at[i]) for i, b in enumerate(blocks)]
    read.append(pltpu.make_async_copy(gh, buf_h, sem_in.at[8]))
    write.append(pltpu.make_async_copy(buf_h, gh_o, sem_out.at[8]))
    for copy in read:
        copy.start()
    loss_o[...] = loss[...]
    for copy, after in zip(read, write):
        copy.wait()
        after.start()
    for copy in write:
        copy.wait()


def fused_shards(student_hidden, head_weight, teacher_logits):
    nv, nh = lax.axis_size("vocab"), lax.axis_size("hid")
    tokens, width = student_hidden.shape
    vw = head_weight.shape[1]
    per = teacher_logits.shape[0]
    half, nz, nq, ncb = per // 2, nv // 2, 4, 2
    nb = nv // 2
    rows, cw, tile = nb * half, width // ncb, width // 4
    hidden = student_hidden.reshape(nz // 2, 2, 2, nh, per, width)
    any_, vmem = pl.BlockSpec(memory_space=pl.ANY), pl.BlockSpec(memory_space=pltpu.VMEM)
    dma = lambda *shape: pltpu.SemaphoreType.DMA(shape)
    steps = nq * ncb
    loss, gh, gw = pl.pallas_call(
        functools.partial(fused, tokens),
        out_shape=(
            jax.ShapeDtypeStruct((1, 1), F32),
            jax.ShapeDtypeStruct((nh, per, width), BF16),
            jax.ShapeDtypeStruct((width, vw), BF16),
        ),
        in_specs=[any_, any_, any_],
        out_specs=(vmem, vmem, any_),
        scratch_shapes=[
            pltpu.VMEM((width, vw), BF16),
            pltpu.VMEM((nh, nq, 2, 2, half, width), BF16),
            pltpu.VMEM((nq, nb, half, vw), BF16),
            pltpu.VMEM((2, nq, rows, vw), F32),
            pltpu.VMEM((2, nq, rows, vw), F32),
            pltpu.VMEM((nq, rows, vw // 2 + 128), F32),
            pltpu.VMEM((nq, rows, vw // 2 + 128), F32),
            pltpu.VMEM((nq, rows, vw), F32),
            pltpu.VMEM((nq, rows, vw), F32),
            pltpu.VMEM((nq, 8, 128), F32),
            pltpu.VMEM((nq, nv, 8, 128), F32),
            pltpu.VMEM((128, 128), F32),
            pltpu.VMEM((8, 128), F32),
            pltpu.VMEM((nh, 8, 128), F32),
            pltpu.VMEM((nh, nq, rows, vw), BF16),
            pltpu.VMEM((nh, 2, 2, half, cw), F32),
            pltpu.VMEM((steps, nh, 2, half, cw), BF16),
            pltpu.VMEM((steps, nh, 2, half, cw), BF16),
            pltpu.VMEM((steps, nh, 2, half, cw), F32),
            pltpu.VMEM((steps, 2, nh, half, cw), BF16),
            pltpu.VMEM((steps, nz, nh, half, cw), BF16),
            pltpu.VMEM((2, tile, vw), BF16),
            pltpu.VMEM((width, nh * nq * rows), BF16),
            dma(nq * nh + 2 + 4),
            dma(2, nv), dma(2, nv), dma(2, nq), dma(2, nq), dma(nq), dma(nq), dma(nq, nv), dma(nq, nv),
            dma(nq, 3), dma(nq, 3), dma(nh), dma(nh), dma(steps), dma(steps), dma(steps, 2), dma(steps, nz),
            dma(2),
        ],
        compiler_params=pltpu.CompilerParams(
            collective_id=0, has_side_effects=True, vmem_limit_bytes=60 * 1024 * 1024
        ),
        cost_estimate=pl.CostEstimate(
            flops=6 * tokens * width * vw, bytes_accessed=4 * width * vw, transcendentals=0
        ),
    )(hidden, head_weight, teacher_logits)
    loss, gh, gw = pl.pallas_call(
        hand_out,
        out_shape=tuple(jax.ShapeDtypeStruct(a.shape, a.dtype) for a in (loss, gh, gw)),
        in_specs=[vmem, any_, any_],
        out_specs=(vmem, any_, any_),
        scratch_shapes=[pltpu.VMEM(gw.shape, BF16), pltpu.VMEM(gh.shape, BF16), dma(9), dma(9)],
        compiler_params=pltpu.CompilerParams(vmem_limit_bytes=60 * 1024 * 1024),
        cost_estimate=pl.CostEstimate(flops=0, bytes_accessed=4 * width * vw, transcendentals=0),
    )(loss, gh, gw)
    return loss.reshape(()), gh.reshape(nh * per, width), gw


def shards(student_hidden, head_weight, teacher_logits):
    n_vocab = lax.axis_size("vocab")
    n_hid = lax.axis_size("hid")
    tokens, width = student_hidden.shape
    vocab_width = head_weight.shape[1]
    per_dev = teacher_logits.shape[0]
    mine = n_vocab * per_dev
    teacher = lax.all_to_all(
        teacher_logits, "vocab", split_axis=1, concat_axis=0, tiled=True
    ).astype(jnp.float32)
    hidden = student_hidden.reshape(n_vocab, n_hid, per_dev, width)
    hidden = hidden.transpose(1, 0, 2, 3).reshape(tokens, width)
    partial_value = jnp.dot(hidden, head_weight, preferred_element_type=jnp.float32)
    logits = lax.psum_scatter(partial_value, "hid", scatter_dimension=0, tiled=True)
    top_s = jnp.max(logits, axis=1, keepdims=True)
    top_t = jnp.max(teacher, axis=1, keepdims=True)
    e = jnp.exp(logits - top_s)
    stats = jnp.stack(
        [
            top_s[:, 0],
            jnp.sum(e, axis=1),
            jnp.sum(e * ((logits - top_s) - (teacher - top_t)), axis=1),
            top_t[:, 0],
            jnp.sum(jnp.exp(teacher - top_t), axis=1),
        ]
    )
    every = lax.all_gather(stats, "vocab", axis=0)
    m_s, s_s, a, m_t, s_t = [every[:, i] for i in range(5)]
    all_s, all_t = jnp.max(m_s, axis=0), jnp.max(m_t, axis=0)
    w = jnp.exp(m_s - all_s)
    total_s = jnp.sum(w * s_s, axis=0)
    total_t = jnp.sum(jnp.exp(m_t - all_t) * s_t, axis=0)
    log_s, log_t = jnp.log(total_s), jnp.log(total_t)
    gap = (m_s - all_s) - (m_t - all_t)
    kl_row = jnp.sum(w * (a + s_s * gap), axis=0) / total_s - log_s + log_t
    loss_value = lax.psum(jnp.sum(kl_row), "hid") / tokens
    student_log = logits - (all_s + log_s)[:, None]
    teacher_log = teacher - (all_t + log_t)[:, None]
    grad = (jnp.exp(student_log) * (student_log - teacher_log - kl_row[:, None]) / tokens).astype(
        jnp.bfloat16
    )
    grad = lax.all_gather(grad, "hid", axis=0, tiled=True)
    grad_hidden = lax.dot_general(
        grad, head_weight, (((1,), (1,)), ((), ())), preferred_element_type=jnp.float32
    ).astype(jnp.bfloat16)
    grad_hidden = grad_hidden.reshape(n_hid, n_vocab, per_dev, width).transpose(1, 0, 2, 3)
    grad_hidden = lax.psum_scatter(
        grad_hidden.reshape(tokens, width), "vocab", scatter_dimension=0, tiled=True
    )
    grad_weight = lax.dot_general(
        hidden, grad, (((0,), (0,)), ((), ())), preferred_element_type=jnp.float32
    ).astype(jnp.bfloat16)
    return (loss_value, grad_hidden, grad_weight)


def solution(mesh):
    fits = mesh.shape["hid"] == 4 and mesh.shape["vocab"] == 8
    def body(student_hidden, head_weight, teacher_logits):
        ok = fits and teacher_logits.shape[0] == 32
        return (fused_shards if ok else shards)(student_hidden, head_weight, teacher_logits)

    in_specs = (P(None, "hid"), P("hid", "vocab"), P(("vocab", "hid"), None))
    out_specs = (P(), P("vocab", "hid"), P("hid", "vocab"))
    return jax.shard_map(body, mesh=mesh, in_specs=in_specs, out_specs=out_specs, check_vma=False)
```
